512 devices in a mesh: dp: 16 (over z, core), fsdp: 4 (over x), tensor: 8 (over y).
Axes of the slice: x: 4, y: 8, z: 8, core: 2. Of those that a mesh axis runs over, the one named last changes fastest.
Arguments:
- tokens: bfloat16 [16384, 8192], P(('dp', 'fsdp'), 'tensor'), may hold values from -700 to 700
- queries: bfloat16 [16384, 8192], P(('dp', 'fsdp'), 'tensor'), may hold values from -140 to 140
- segment_ids: int32 [128, 128], P(('dp', 'fsdp')), may hold values from 0 to 3, never falling along the last dimension, each value on 1 to 64 neighbouring positions
- gain: float32 [8192], P('tensor'), may hold values from 0.1 to 1.9
- key_value_weight: bfloat16 [8192, 2048], P('tensor', 'fsdp'), may hold values from -0.0625 to 0.0625
- plan: int32 [32], replicated, may hold values from 0 to 31, as said below
Outputs:
- attended: bfloat16 [16384, 8192], P(('dp', 'fsdp'), 'tensor')
The draws below stay inside these ranges and needn't reach their ends.
Inputs may be any that keep to these rules, and one draw needn't show every extreme that they name: plan is a permutation of 0 to 31; from one dp index to another at most 1 micro-batches go, and in every draw some pair of dp indices carries exactly 1.
All inputs are finite; a program needn't handle non-finite values.
Results may differ from the reference program's by a relative error of at most 0.011.
Values may be sent and summed in bfloat16 or wider, within the bound.
No kernel may reach another device: no remote copies, remote signals or barrier semaphores. Data moves between devices by JAX's collectives and lax.ppermute only.
A program may use at most 64 MiB of HBM per device.

```python
import math
import jax
import jax.numpy as jnp
import numpy as np
from jax import lax

MODEL_WIDTH = 8192
QUERY_HEADS = 64
KEY_VALUE_HEADS = 8
HEAD_SIZE = 128
MICRO_TOKENS = 128
MB_DEV = 2
CAP = 1
MICRO = 32
BATCHES = 128
TOKENS = 16384
N_DP = 16
N_FSDP = 4


def draw_tokens(key, part):
    keys = jax.random.split(key, 3)
    columns = jnp.arange(MODEL_WIDTH, dtype=jnp.float32) / MODEL_WIDTH
    base = jnp.clip(jax.random.normal(keys[0], (TOKENS, MODEL_WIDTH), jnp.float32), -4.0, 4.0)
    ramp = jnp.sqrt(1.0 + 2.0 * columns)
    row_scale = jnp.exp(jax.random.uniform(keys[1], (TOKENS, 1), minval=0.0, maxval=math.log(10.0)))
    column_scale = jnp.exp(jax.random.uniform(keys[2], (1, MODEL_WIDTH), minval=0.0, maxval=math.log(10.0))) * ramp[None, :]
    return (base * row_scale * column_scale).astype(jnp.bfloat16)


def draw_queries(key, part):
    keys = jax.random.split(key, 1)
    values = jnp.clip(jax.random.normal(keys[0], (TOKENS, QUERY_HEADS * HEAD_SIZE), jnp.float32), -4.0, 4.0)
    return values.astype(jnp.bfloat16)


def draw_plan(key, part):
    keys = jax.random.split(key, 4)
    offsets = jax.random.permutation(keys[0], N_DP)
    arrangement = jax.random.permutation(keys[1], MB_DEV)
    shifting = offsets[arrangement // CAP]
    target_slot = jax.random.permutation(keys[2], MB_DEV)
    relabel = jax.random.permutation(keys[3], N_DP)
    relabel_back = jnp.argsort(relabel)
    sources = jnp.arange(N_DP, dtype=jnp.int32)
    target_rank = relabel[(relabel_back[sources][:, None] + shifting[None, :]) % N_DP]
    layout = target_rank * MB_DEV + target_slot[None, :]
    return layout.reshape(MICRO).astype(jnp.int32)


def block_levels(own_key, dims, pieces, smallest, high):
    def one(position, parts):
        heights = jax.random.uniform(jax.random.fold_in(jax.random.fold_in(own_key, 6), position), (parts,), jnp.float32, smallest / len(pieces), high / len(pieces))
        return jnp.repeat(jnp.exp(heights), dims[position] // parts).reshape((-1,) + (1,) * (len(dims) - position - 1))

    level = one(*pieces[0])
    for cut in pieces[1:]:
        level = level * one(*cut)
    return level


def profile(number_of, total, bound, skew):
    weights = [(1 << 20) // math.isqrt(standing ** skew) + 1 for standing in range(2, number_of + 1)]
    rest, counts = total - bound - (number_of - 1), [1] * (number_of - 1)
    while rest > 0:
        movable = [i for i in range(number_of - 1) if counts[i] < bound]
        whole, left = sum([weights[i] for i in movable]), rest
        for i in movable:
            addition = min(bound - counts[i], max(1, left * weights[i] // whole), rest)
            counts[i] = counts[i] + addition
            rest = rest - addition
    return np.array([bound] + counts)


def ragged(rng, count, total, most, skew):
    if count == 2:
        one = jax.random.randint(rng, (), max(1, total - most), min(most, total - 1) + 1)
        return jnp.stack([one, total - one])
    lengths = jnp.asarray(profile(count, total, most, skew), jnp.int32)
    couples = (count - 1) // 2
    source_of, taker = lengths[1:1 + 2 * couples:2], lengths[2:2 + 2 * couples:2]
    margin = jnp.minimum(source_of - 1, most - taker)
    moved = jax.random.randint(jax.random.fold_in(rng, 1), (couples,), 0, 1 << 20) % (margin + 1)
    lengths = lengths.at[1:1 + 2 * couples:2].set(source_of - moved).at[2:2 + 2 * couples:2].set(taker + moved)
    return lengths[jax.random.permutation(jax.random.fold_in(rng, 2), count)]


def noise(rng, extent, spread, limit, pieces=(), held_as=jnp.bfloat16):
    loudness = block_levels(rng, extent, pieces, -0.22, 0.18) if pieces else 1.0
    values = jax.random.normal(rng, extent, jnp.float32) * spread * loudness
    return jnp.minimum(jnp.maximum(values, -limit), limit).astype(held_as)


def setup_inputs(seed: int = 0) -> dict:
    key_of = jax.random.split(jax.random.key(seed), 7)
    tokens = draw_tokens(jax.random.fold_in(key_of[6], 71), 0)
    queries = draw_queries(jax.random.fold_in(key_of[6], 71), 0)
    segment_ids = jax.vmap(lambda own: jnp.searchsorted(jnp.cumsum(ragged(own, 4, MICRO_TOKENS, MICRO_TOKENS // 2, 1)), jnp.arange(MICRO_TOKENS), side="right"))(jax.random.split(key_of[2], BATCHES)).reshape((BATCHES, MICRO_TOKENS)).astype(jnp.int32)
    gain = jnp.clip(1.0 + 0.18 * jax.random.normal(key_of[3], (MODEL_WIDTH,), jnp.float32), 0.1, 1.9)
    key_value_weight = noise(key_of[4], (MODEL_WIDTH, 2 * KEY_VALUE_HEADS * HEAD_SIZE), MODEL_WIDTH ** -0.5, 0.0625, ((0, 8), (1, 4)))
    plan = draw_plan(jax.random.fold_in(key_of[6], 71), 0)
    return dict(tokens=tokens, queries=queries, segment_ids=segment_ids, gain=gain, key_value_weight=key_value_weight, plan=plan)


epsilon = 1e-05

def attend_block(query_block, key_block, value_block, doc_block):
    scores = jnp.einsum('qhgd,khd->hgqk', query_block, key_block, precision=lax.Precision.HIGHEST) * HEAD_SIZE ** (-0.5)
    positions = jnp.arange(MICRO_TOKENS, dtype=jnp.int32)
    allowed = (doc_block[:, None] == doc_block[None, :]) & (positions[:, None] >= positions[None, :])
    scores = jnp.where(allowed[None, None], scores, -1e+30)
    row_max = lax.optimization_barrier(jnp.max(scores, axis=-1, keepdims=True))
    expo = jnp.exp(scores - row_max)
    weights = (expo / lax.optimization_barrier(jnp.sum(expo, axis=-1, keepdims=True))).astype(jnp.bfloat16)
    mixed = jnp.einsum('hgqk,khd->qhgd', weights.astype(jnp.float32), value_block, precision=lax.Precision.HIGHEST)
    return mixed.reshape(MICRO_TOKENS, QUERY_HEADS * HEAD_SIZE).astype(jnp.bfloat16)

def reference(tokens, queries, segment_ids, gain, key_value_weight, plan):
    complete_weight = key_value_weight.astype(jnp.float32)
    head_group = QUERY_HEADS // KEY_VALUE_HEADS

    def one_block(item):
        rows, query_row_block, doc_row = item
        values = rows.astype(jnp.float32)
        scale = lax.rsqrt(lax.optimization_barrier(jnp.sum(values * values, axis=1)) / MODEL_WIDTH + epsilon)
        normed = (values * scale[:, None] * gain).astype(jnp.bfloat16)
        key_value_rows = jnp.dot(normed.astype(jnp.float32), complete_weight, precision=lax.Precision.HIGHEST)
        key_value_heads = key_value_rows.reshape(MICRO_TOKENS, KEY_VALUE_HEADS, 2, HEAD_SIZE)
        query_head_count = query_row_block.astype(jnp.float32).reshape(MICRO_TOKENS, KEY_VALUE_HEADS, head_group, HEAD_SIZE)
        return attend_block(query_head_count, key_value_heads[:, :, 0], key_value_heads[:, :, 1], doc_row)
    blocks = lax.map(one_block, (tokens.reshape(BATCHES, MICRO_TOKENS, MODEL_WIDTH), queries.reshape(BATCHES, MICRO_TOKENS, QUERY_HEADS * HEAD_SIZE), segment_ids))
    grid = blocks.reshape(N_DP, N_FSDP, MB_DEV, MICRO_TOKENS, QUERY_HEADS * HEAD_SIZE).transpose(1, 0, 2, 3, 4).reshape(N_FSDP, MICRO, MICRO_TOKENS, QUERY_HEADS * HEAD_SIZE)
    inverse = jnp.argsort(plan).astype(jnp.int32)
    moved = grid[:, inverse]
    return moved.reshape(N_FSDP, N_DP, MB_DEV, MICRO_TOKENS, QUERY_HEADS * HEAD_SIZE).transpose(1, 0, 2, 3, 4).reshape(TOKENS, QUERY_HEADS * HEAD_SIZE)
```

```python
import functools
import jax
import jax.numpy as jnp
from jax import lax
from jax.experimental import pallas as pl
from jax.experimental.pallas import tpu as pltpu
from jax.sharding import PartitionSpec as P

HEAD_SIZE = 128
EPSILON = 1e-05
VMEM = pl.BlockSpec(memory_space=pltpu.VMEM)
SMEM = pl.BlockSpec(memory_space=pltpu.SMEM)


def call(kernel, out_shape, in_specs, scratch, flops, moved, limit=24 << 20):
    return pl.pallas_call(
        kernel,
        out_shape=out_shape,
        in_specs=in_specs,
        out_specs=jax.tree.map(lambda _: VMEM, out_shape),
        scratch_shapes=scratch,
        compiler_params=pltpu.CompilerParams(vmem_limit_bytes=limit),
        cost_estimate=pl.CostEstimate(flops=flops, bytes_accessed=moved, transcendentals=0),
    )


def place_queries_kernel(plan, arrived, out, stage):
    ranks = arrived.shape[0]
    for p in range(ranks):
        rows = arrived[p, 16:32, :].astype(jnp.float32)
        for s in range(2):
            stage[pl.ds(pl.multiple_of(plan[2 * p + s] * 8, 8), 8), :] = rows[s * 8:s * 8 + 8]
    out[...] = stage[...].astype(jnp.bfloat16).reshape(out.shape)


def project_kernel(plan, place, arrived, scale, gain, own, right, left, far_a, far_b,
                   right_o, left_o, far_ao, far_bo, out, stage, normed):
    ranks = arrived.shape[0]
    half = normed.shape[2]
    quarter = half // 2
    for p in range(ranks):
        rows = arrived[p, 0:16, :].astype(jnp.float32)
        rows = rows * scale[p * 16:p * 16 + 16, :] * gain[...]
        for s in range(2):
            stage[pl.ds(pl.multiple_of(plan[2 * p + s] * 8, 8), 8), :] = rows[s * 8:s * 8 + 8]
    for i in range(2):
        normed[i] = stage[:, i * half:(i + 1) * half].astype(jnp.bfloat16)
    core = place[0]
    shard = place[1]

    def dot(a, b):
        return jnp.dot(a, b, preferred_element_type=jnp.float32)

    def put(index, total):
        blocks = total.astype(jnp.bfloat16).reshape(ranks, 16, 2 * 2 * HEAD_SIZE)
        for h in range(2):
            out[:, index * 2 + h] = blocks[:, :, h * 2 * HEAD_SIZE:(h + 1) * 2 * HEAD_SIZE]

    put(shard, dot(normed[0], own[:half, :]) + dot(normed[1], own[half:, :]))
    mine, other = normed.at[core], normed.at[1 - core]
    put(lax.rem(shard + 3, 4), dot(mine[...], right[...]) + dot(other[...], right_o[...]))
    put(lax.rem(shard + 1, 4), dot(mine[...], left[...]) + dot(other[...], left_o[...]))
    put(
        lax.rem(shard + 2, 4),
        dot(mine[:, :quarter], far_a[...]) + dot(mine[:, quarter:], far_b[...])
        + dot(other[:, :quarter], far_ao[...]) + dot(other[:, quarter:], far_bo[...]),
    )


def attend_kernel(parts, queries, seg_row, seg_col, out, key_value):
    groups = 8
    ranks = queries.shape[0]
    length = key_value.shape[1]
    for i in range(ranks):
        total = parts[i * groups].astype(jnp.float32)
        for k in range(1, groups):
            total = total + parts[i * groups + k].astype(jnp.float32)
        for s in range(2):
            key_value[s, i * 8:i * 8 + 8, :] = total[s * 8:s * 8 + 8]
    rows = lax.broadcasted_iota(jnp.int32, (length, length), 0)
    columns = lax.broadcasted_iota(jnp.int32, (length, length), 1)
    wide = queries[...].astype(jnp.float32).reshape(ranks, 2, 8, queries.shape[2])
    for s in range(2):
        allowed = (seg_col[s * length:(s + 1) * length, :] == seg_row[s:s + 1, :]) & (columns <= rows)
        key = key_value[s, :, :HEAD_SIZE]
        value = key_value[s, :, HEAD_SIZE:]
        key_high = key.astype(jnp.bfloat16)
        key_low = (key - key_high.astype(jnp.float32)).astype(jnp.bfloat16)
        value_high = value.astype(jnp.bfloat16)
        value_low = (value - value_high.astype(jnp.float32)).astype(jnp.bfloat16)
        query = wide[:, s].reshape(length, queries.shape[2]).astype(jnp.bfloat16)
        for n in range(groups):
            at = query[:, n * HEAD_SIZE:(n + 1) * HEAD_SIZE]
            turned = (((1,), (1,)), ((), ()))
            scores = lax.dot_general(at, key_high, turned, preferred_element_type=jnp.float32)
            scores = scores + lax.dot_general(at, key_low, turned, preferred_element_type=jnp.float32)
            scores = jnp.where(allowed, scores * HEAD_SIZE ** (-0.5), -1e30)
            expo = jnp.exp(scores - jnp.max(scores, axis=1, keepdims=True))
            weights = (expo / jnp.sum(expo, axis=1, keepdims=True)).astype(jnp.bfloat16)
            mixed = jnp.dot(weights, value_high, preferred_element_type=jnp.float32)
            mixed = mixed + jnp.dot(weights, value_low, preferred_element_type=jnp.float32)
            out[s * length:(s + 1) * length, n * HEAD_SIZE:(n + 1) * HEAD_SIZE] = mixed.astype(jnp.bfloat16)


def gather_weight(weight, core):
    half = weight.shape[0] // 2
    up = [(i, (i + 1) % 4) for i in range(4)]
    down = [(i, (i + 3) % 4) for i in range(4)]
    swap = [(i, i ^ 1) for i in range(16)]
    mine = lax.dynamic_slice_in_dim(weight, core * half, half, 0)
    right = lax.ppermute(mine, "fsdp", up)
    left = lax.ppermute(mine, "fsdp", down)
    far_a = lax.ppermute(right[:half // 2], "fsdp", up)
    far_b = lax.ppermute(left[half // 2:], "fsdp", down)
    held = (right, left, far_a, far_b)
    return held + tuple(lax.ppermute(a, "dp", swap) for a in held)


def shards(tokens, queries, segment_ids, gain, weight, plan):
    ranks = lax.axis_size("dp")
    groups = lax.axis_size("tensor")
    rank = lax.axis_index("dp")
    width = tokens.shape[1]
    slots, length = segment_ids.shape
    core = lax.rem(rank, 2)
    place = jnp.stack([core, lax.axis_index("fsdp")]).astype(jnp.int32)

    def cut(a):
        return a.reshape(slots, ranks, 8, width).transpose(1, 0, 2, 3)

    first = jnp.concatenate([cut(tokens), cut(queries)], axis=1)
    arrived = lax.all_to_all(first, "dp", 0, 0, tiled=True).reshape(ranks, 32, width)
    pieces = gather_weight(weight, core)

    values = tokens.astype(jnp.float32)
    sums = jnp.sum(values * values, axis=1).reshape(slots, length)
    facts = jnp.stack([sums, segment_ids.astype(jnp.float32)])
    facts = lax.all_gather(facts, ("dp", "tensor")).reshape(ranks, groups, 2, slots, length)
    totals = facts[:, :, 0].sum(axis=1).reshape(ranks * slots, length)
    scale = lax.rsqrt(totals / (width * groups) + EPSILON)
    scale = lax.dynamic_slice_in_dim(scale, rank * 8, 8, 1).reshape(ranks * slots * 8, 1)
    goal = rank * slots + jnp.arange(slots, dtype=jnp.int32)
    here = (plan[None, :] == goal[:, None]).astype(jnp.float32)
    documents = facts[:, 0, 1].reshape(ranks * slots, length)
    documents = (here[:, :, None] * documents[None]).sum(axis=1)

    placed = call(
        place_queries_kernel,
        jax.ShapeDtypeStruct((ranks, 16, width), jnp.bfloat16),
        [SMEM, VMEM],
        [pltpu.VMEM((ranks * 16, width), jnp.float32)],
        0, 2 << 20,
    )(plan, arrived)
    placed = lax.all_to_all(placed, "dp", 0, 0, tiled=True)

    rows = ranks * 16
    parts = call(
        project_kernel,
        jax.ShapeDtypeStruct((ranks, groups, 16, 2 * HEAD_SIZE), jnp.bfloat16),
        [SMEM, SMEM] + [VMEM] * 12,
        [pltpu.VMEM((rows, width), jnp.float32), pltpu.VMEM((2, rows, width // 2), jnp.bfloat16)],
        2 * rows * width * groups * 2 * HEAD_SIZE, 8 << 20,
    )(plan, place, arrived, scale, gain.reshape(1, width), weight, *pieces)
    parts = lax.all_to_all(
        parts.reshape(ranks * groups, 16, 2 * HEAD_SIZE), ("dp", "tensor"), 0, 0, tiled=True
    )

    return call(
        attend_kernel,
        jax.ShapeDtypeStruct((slots * length, width), jnp.bfloat16),
        [VMEM] * 4,
        [pltpu.VMEM((slots, length, 2 * HEAD_SIZE), jnp.float32)],
        8 * slots * 8 * length * length * HEAD_SIZE, 4 << 20,
    )(parts, placed, documents, documents.reshape(slots * length, 1))


def solution(mesh):
    placed = (
        P(("dp", "fsdp"), "tensor"),
        P(("dp", "fsdp"), "tensor"),
        P(("dp", "fsdp"), None),
        P("tensor"),
        P("tensor", "fsdp"),
        P(),
    )
    return jax.shard_map(
        shards, mesh=mesh, in_specs=placed, out_specs=P(("dp", "fsdp"), "tensor"), check_vma=False
    )
```
